32 devices in a mesh: grp: 2 (over y), row: 4 (over z), col: 4 (over x, core).
Axes of the slice: x: 2, y: 2, z: 4, core: 2. Of those that a mesh axis runs over, the one named last changes fastest.
Arguments:
- pair: bfloat16 [128, 64, 128], P(('grp', 'row'), 'col'), parts along dimension 0, may hold values from -6 to 6
- cotangent: bfloat16 [128, 64, 128], P(('grp', 'row'), 'col'), parts along dimension 0, may hold values from -6 to 6
- lengths: int32 [2], P('grp'), parts along dimension 0, may hold values from 32 to 64
- norm_in_gain: float32 [128], replicated, may hold values from 0.25 to 1.75
- norm_in_bias: float32 [128], replicated, may hold values from -3 to 3
- left_weight: bfloat16 [128, 256], replicated, may hold values from -0.5 to 0.5
- right_weight: bfloat16 [128, 256], replicated, may hold values from -0.5 to 0.5
- gate_weight: bfloat16 [128, 128], replicated, may hold values from -0.5 to 0.5
- norm_mid_gain: float32 [128], replicated, may hold values from 0.25 to 1.75
- norm_mid_bias: float32 [128], replicated, may hold values from -3 to 3
- out_weight: bfloat16 [128, 128], replicated, may hold values from -0.5 to 0.5
Outputs:
- result: bfloat16 [128, 64, 128], P(('grp', 'row'), 'col'), parts along dimension 0
- grad_pair: float32 [128, 64, 128], P(('grp', 'row'), 'col'), parts along dimension 0
- d_left: float32 [256, 256], P('grp'), parts along dimension 0
- d_right: float32 [256, 256], P('grp'), parts along dimension 0
- d_gate: float32 [256, 128], P('grp'), parts along dimension 0
- d_out: float32 [256, 128], P('grp'), parts along dimension 0
- d_norm_in: float32 [4, 128], P('grp'), parts along dimension 0
- d_norm_mid: float32 [4, 128], P('grp'), parts along dimension 0
The draws below stay inside these ranges and needn't reach their ends.
There are 2 independent parts, one for each index of `grp`. The reference program is written for one: setup_inputs(seed, part) draws one part's arguments, and reference() takes and returns one part's arrays. A program takes and returns all parts, laid end to end along the dimension named above; an argument that names none is the same for every part. Nothing has to cross between parts.
All inputs are finite; a program needn't handle non-finite values.
Results may differ from the reference program's by a relative error of at most 0.0072.
Values may be sent and summed in bfloat16 or wider, within the bound.
A program may use at most 64 MiB of HBM per device.

```python
import jax
import jax.numpy as jnp
from jax import lax

C = 128
H = 128
TOKENS = 64


def shard_levels(key, extent, cuts, least, high):
    def one(dim, blocks):
        steps = jax.random.uniform(jax.random.fold_in(jax.random.fold_in(key, 6), dim), (blocks,), jnp.float32, least / len(cuts), high / len(cuts))
        return jnp.repeat(jnp.exp(steps), extent[dim] // blocks).reshape((-1,) + (1,) * (len(extent) - dim - 1))

    level = one(*cuts[0])
    for cut in cuts[1:]:
        level = level * one(*cut)
    return level


def noise(key, extent, scale, reach, cuts=(), held_as=jnp.bfloat16):
    entries = scale * jax.random.normal(key, extent, jnp.float32)
    if cuts:
        entries = entries * shard_levels(key, extent, cuts, -0.22, 0.18)
    return jnp.clip(entries, -reach, reach).astype(held_as)


def setup_inputs(seed: int = 0, part: int = 0) -> dict:
    key_of = jax.random.split(jax.random.key(seed), 12)
    part_splits = jax.random.split(jax.random.fold_in(key_of[11], part), 12)
    pair = noise(part_splits[0], (TOKENS, TOKENS, C), 1.0, 6.0, ((0, 4), (1, 4)))
    cotangent = noise(part_splits[1], (TOKENS, TOKENS, C), 1.0, 6.0, ((0, 4), (1, 4)))
    lengths = jax.random.randint(part_splits[2], (1,), TOKENS // 2, TOKENS + 1).astype(jnp.int32)
    norm_in_gain = jnp.clip(1.0 + 0.15 * jax.random.normal(key_of[3], (C,), jnp.float32), 0.25, 1.75)
    norm_in_bias = noise(key_of[4], (C,), 0.5, 3.0, (), jnp.float32)
    left_weight = noise(key_of[5], (C, 2 * H), C ** -0.5, 0.5)
    right_weight = noise(key_of[6], (C, 2 * H), C ** -0.5, 0.5)
    gate_weight = noise(key_of[7], (C, C), C ** -0.5, 0.5)
    norm_mid_gain = jnp.clip(1.0 + 0.15 * jax.random.normal(key_of[8], (H,), jnp.float32), 0.25, 1.75)
    norm_mid_bias = noise(key_of[9], (H,), 0.5, 3.0, (), jnp.float32)
    out_weight = noise(key_of[10], (H, C), H ** -0.5, 0.5)
    return {"pair": pair, "cotangent": cotangent, "lengths": lengths, "norm_in_gain": norm_in_gain, "norm_in_bias": norm_in_bias, "left_weight": left_weight, "right_weight": right_weight, "gate_weight": gate_weight, "norm_mid_gain": norm_mid_gain, "norm_mid_bias": norm_mid_bias, "out_weight": out_weight}


EPS = 1e-05

def normalize(value, gain, bias):
    centre = value - lax.optimization_barrier(jnp.mean(value, axis=-1, keepdims=True))
    spread = lax.rsqrt(lax.optimization_barrier(jnp.mean(centre * centre, axis=-1, keepdims=True)) + EPS)
    scaled = centre * spread
    return (scaled * gain + bias, scaled, spread)

def norm_back(upstream, gain, scaled, spread):
    inner_grad = upstream * gain
    centred = inner_grad - lax.optimization_barrier(jnp.mean(inner_grad, axis=-1, keepdims=True))
    return spread * (centred - scaled * lax.optimization_barrier(jnp.mean(inner_grad * scaled, axis=-1, keepdims=True)))

def gated_half(normed, weight, pair_mask):
    projected = jnp.dot(normed, weight, preferred_element_type=jnp.float32)
    half_width = weight.shape[1] // 2
    values = projected[..., :half_width]
    switch = jax.nn.sigmoid(projected[..., half_width:])
    return (pair_mask * switch * values, values, switch)

def gated_back(upstream, pair_mask, values, switch):
    first = upstream * pair_mask * switch
    second = upstream * pair_mask * values * switch * (1.0 - switch)
    return jnp.concatenate([first, second], axis=-1).astype(jnp.bfloat16)

def cell_sum(first, second):
    return jnp.einsum('ijc,ijh->ch', first.astype(jnp.float32), second.astype(jnp.float32))

def reference(pair, cotangent, lengths, norm_in_gain, norm_in_bias, left_weight, right_weight, gate_weight, norm_mid_gain, norm_mid_bias, out_weight):
    tokens_all = pair.shape[0]
    normed, scaled_in, spread_in = normalize(pair.astype(jnp.float32), norm_in_gain, norm_in_bias)
    normed_b = normed.astype(jnp.bfloat16)
    valid = (jnp.arange(tokens_all, dtype=jnp.int32) < lengths[0]).astype(jnp.float32)
    pair_mask = valid[:, None, None] * valid[None, :, None]
    left, left_values, left_switch = gated_half(normed_b, left_weight, pair_mask)
    right, right_values, right_switch = gated_half(normed_b, right_weight, pair_mask)
    left_b = left.astype(jnp.bfloat16)
    right_b = right.astype(jnp.bfloat16)
    product = jnp.einsum('ikh,jkh->ijh', left_b.astype(jnp.float32), right_b.astype(jnp.float32))
    mixed, scaled_mid, spread_mid = normalize(product, norm_mid_gain, norm_mid_bias)
    mixed_b = mixed.astype(jnp.bfloat16)
    update = jnp.dot(mixed_b, out_weight, preferred_element_type=jnp.float32)
    switch_out = jax.nn.sigmoid(jnp.dot(normed_b, gate_weight, preferred_element_type=jnp.float32))
    result = (switch_out * update).astype(jnp.bfloat16)
    upstream = cotangent.astype(jnp.float32)
    grad_update = (upstream * switch_out).astype(jnp.bfloat16)
    grad_gate = (upstream * update * switch_out * (1.0 - switch_out)).astype(jnp.bfloat16)
    grad_mixed = jnp.dot(grad_update, out_weight.T, preferred_element_type=jnp.float32)
    grad_product = norm_back(grad_mixed, norm_mid_gain, scaled_mid, spread_mid).astype(jnp.bfloat16)
    grad_left = jnp.einsum('ijh,jkh->ikh', grad_product.astype(jnp.float32), right_b.astype(jnp.float32))
    grad_right = jnp.einsum('ijh,ikh->jkh', grad_product.astype(jnp.float32), left_b.astype(jnp.float32))
    left_back = gated_back(grad_left, pair_mask, left_values, left_switch)
    right_back = gated_back(grad_right, pair_mask, right_values, right_switch)
    grad_normed = jnp.dot(left_back, left_weight.T, preferred_element_type=jnp.float32)
    grad_normed = grad_normed + jnp.dot(right_back, right_weight.T, preferred_element_type=jnp.float32)
    grad_normed = grad_normed + jnp.dot(grad_gate, gate_weight.T, preferred_element_type=jnp.float32)
    grad_pair = norm_back(grad_normed, norm_in_gain, scaled_in, spread_in)
    factor = 1.0 / tokens_all
    d_left = cell_sum(normed_b, left_back) * factor
    d_right = cell_sum(normed_b, right_back) * factor
    d_gate = cell_sum(normed_b, grad_gate) * factor
    d_out = cell_sum(mixed_b, grad_update) * factor
    d_norm_in = jnp.stack([lax.optimization_barrier(jnp.sum(grad_normed * scaled_in, axis=(0, 1))), lax.optimization_barrier(jnp.sum(grad_normed, axis=(0, 1)))]) * factor
    d_norm_mid = jnp.stack([lax.optimization_barrier(jnp.sum(grad_mixed * scaled_mid, axis=(0, 1))), lax.optimization_barrier(jnp.sum(grad_mixed, axis=(0, 1)))]) * factor
    return (result, grad_pair, d_left, d_right, d_gate, d_out, d_norm_in, d_norm_mid)
```

```python
import functools

import jax
import jax.numpy as jnp
from jax import lax
from jax.experimental import pallas as pl
from jax.experimental.pallas import tpu as pltpu
from jax.sharding import PartitionSpec as P

EPS = 1e-05
MESH = pl.DeviceIdType.MESH
F32 = jnp.float32
BF16 = jnp.bfloat16
EXTRA = 16


def normalize(value, gain, bias):
    centre = value - jnp.mean(value, axis=-1, keepdims=True)
    spread = lax.rsqrt(jnp.mean(centre * centre, axis=-1, keepdims=True) + EPS)
    scaled = centre * spread
    return scaled * gain + bias, scaled, spread


def norm_back(upstream, gain, scaled, spread):
    inner = upstream * gain
    centred = inner - jnp.mean(inner, axis=-1, keepdims=True)
    return spread * (centred - scaled * jnp.mean(inner * scaled, axis=-1, keepdims=True))


def dot(a, b):
    return jnp.dot(a, b, preferred_element_type=F32)


def dot_t(a, b):
    return lax.dot_general(a, b, (((1,), (1,)), ((), ())), preferred_element_type=F32)


def cell_sum(a, b):
    return lax.dot_general(a, b, (((0,), (0,)), ((), ())), preferred_element_type=F32)


def pack_pair(first, second):
    place = lax.broadcasted_iota(jnp.int32, (EXTRA, first.shape[-1]), 0)
    lead_1, lead_2 = first.astype(BF16).astype(F32), second.astype(BF16).astype(F32)
    packed = jnp.where(place == 0, lead_1, 0.0)
    packed = jnp.where(place == 1, lead_2, packed)
    packed = jnp.where(place == 2, first - lead_1, packed)
    packed = jnp.where(place == 3, second - lead_2, packed)
    return packed.astype(BF16)


def unpack_pair(rows):
    return rows[0:1] + rows[2:3], rows[1:2] + rows[3:4]


def kernel(
    n,
    lengths_ref, pair_ref, cot_ref, in_gain_ref, in_bias_ref, left_w_ref, right_w_ref, gate_w_ref,
    mid_gain_ref, mid_bias_ref, out_w_ref,
    result_ref, grad_pair_ref, d_left_ref, d_right_ref, d_gate_ref, d_out_ref, d_in_ref, d_mid_ref,
    left_buf, right_own, right_buf, left_f, right_f, prod_ref, gp_ref,
    gl_out, gl_in, gr_out, gr_in,
    a_src, a_in, a_mid, a_fin, b_src, b_in, b_mid, b_fin,
    l_send, l_recv, r_send, r_recv, gl_send, gl_recv, gr_send, gr_recv,
    a1_send, a1_recv, a2_send, a2_recv, a3_send, a3_recv,
    b1_send, b1_recv, b2_send, b2_recv, b3_send, b3_recv,
):
    block, _, width = pair_ref.shape
    cells = block * block
    row, col = lax.axis_index("row"), lax.axis_index("col")
    everyone = n * n

    def remote(src, dst, send, recv, to_row, to_col):
        return pltpu.make_async_remote_copy(
            src_ref=src, dst_ref=dst, send_sem=send, recv_sem=recv,
            device_id={"row": to_row, "col": to_col}, device_id_type=MESH,
        )

    def peers(body, first=1):
        def step(d, carry):
            body(d)
            return carry

        lax.fori_loop(first, n, step, 0)

    barrier = pltpu.get_barrier_semaphore()

    def greet(d, carry):
        other = lax.rem(row * n + col + d, everyone)
        pl.semaphore_signal(
            barrier, inc=1, device_id={"row": other // n, "col": lax.rem(other, n)}, device_id_type=MESH
        )
        return carry

    lax.fori_loop(1, everyone, greet, 0)

    cell = lax.broadcasted_iota(jnp.int32, (cells, 1), 0)
    count = lengths_ref[0]
    mask = jnp.where(
        (row * block + cell // block < count) & (col * block + cell % block < count), 1.0, 0.0
    ).astype(F32)
    in_gain, in_bias = in_gain_ref[...], in_bias_ref[...]
    normed, scaled_in, spread_in = normalize(
        pair_ref[...].reshape(cells, width).astype(F32), in_gain, in_bias
    )
    normed_b = normed.astype(BF16)

    right_all = dot(normed_b, right_w_ref[...])
    half = right_all.shape[1] // 2
    right_values, right_switch = right_all[:, :half], jax.nn.sigmoid(right_all[:, half:])
    right_gate = mask * right_switch
    right_b = (right_gate * right_values).astype(BF16).reshape(block, block, half)
    right_own[...] = right_b

    @pl.when(row == col)
    def _():
        right_buf[col] = right_b

    pl.semaphore_wait(barrier, everyone - 1)

    def right_copy(d):
        to_row = lax.rem(row + d, n)
        return remote(right_own, right_buf.at[col], r_send.at[d], r_recv.at[col], to_row, row)

    peers(lambda d: right_copy(d).start())

    @pl.when(row != col)
    def _():
        right_copy(0).start()

    left_all = dot(normed_b, left_w_ref[...])
    left_values, left_switch = left_all[:, :half], jax.nn.sigmoid(left_all[:, half:])
    left_gate = mask * left_switch
    left_buf[col] = (left_gate * left_values).astype(BF16).reshape(block, block, half)

    def left_copy(d):
        to_col = lax.rem(col + d, n)
        return remote(left_buf.at[col], left_buf.at[col], l_send.at[d], l_recv.at[col], row, to_col)

    peers(lambda d: left_copy(d).start())

    switch_out = jax.nn.sigmoid(dot(normed_b, gate_w_ref[...]))
    upstream = cot_ref[...].reshape(cells, width).astype(F32)
    grad_update = (upstream * switch_out).astype(BF16)
    grad_mixed = dot_t(grad_update, out_w_ref[...])

    def arrived(buf, recv, slot):
        remote(buf.at[slot], buf.at[slot], recv.at[slot], recv.at[slot], row, col).wait_recv()

    def left_in(d):
        arrived(left_buf, l_recv, lax.rem(col + d, n))

    peers(left_in)
    left_f[...] = left_buf[...].astype(F32)

    def right_in(slot):
        @pl.when((row != col) | (slot != col))
        def _():
            arrived(right_buf, r_recv, slot)

    peers(right_in, 0)
    right_f[...] = right_buf[...].astype(F32)

    def product_row(i, carry):
        near = left_f[:, i]
        rows = []
        for j in range(block):
            rows.append(jnp.sum(jnp.sum(near * right_f[:, j], axis=0), axis=0, keepdims=True))
        prod_ref[i] = jnp.concatenate(rows, axis=0)
        return carry

    lax.fori_loop(0, block, product_row, 0)

    mid_gain = mid_gain_ref[...]
    mixed, scaled_mid, spread_mid = normalize(
        prod_ref[...].reshape(cells, half), mid_gain, mid_bias_ref[...]
    )
    mixed_b = mixed.astype(BF16)
    grad_prod = norm_back(grad_mixed, mid_gain, scaled_mid, spread_mid).astype(BF16).astype(F32)
    gp_ref[...] = grad_prod.reshape(block, block, half)

    def gr_copy(d):
        to_col = lax.rem(col + d, n)
        return remote(gr_out.at[to_col], gr_in.at[row], gr_send.at[d], gr_recv.at[row], col, to_col)

    def gr_block(d):
        at = lax.rem(col + d, n)

        def one(j, carry):
            total = gp_ref[0, pl.ds(j, 1), :] * left_f[at, 0]
            for i in range(1, block):
                total = total + gp_ref[i, pl.ds(j, 1), :] * left_f[at, i]
            gr_out[at, j] = total.astype(BF16)
            return carry

        lax.fori_loop(0, block, one, 0)

    def gr_step(d):
        gr_block(d)
        gr_copy(d).start()

    peers(gr_step)
    gr_block(0)

    @pl.when(row == col)
    def _():
        gr_in[row] = gr_out[col]

    @pl.when(row != col)
    def _():
        gr_copy(0).start()

    def gl_copy(d):
        to_col = lax.rem(col + d, n)
        return remote(gl_out.at[to_col], gl_in.at[col], gl_send.at[d], gl_recv.at[col], row, to_col)

    def gl_block(d, into, slot):
        at = lax.rem(col + d, n)

        def one(i, carry):
            total = gp_ref[i, 0:1, :] * right_f[at, 0]
            for j in range(1, block):
                total = total + gp_ref[i, j : j + 1, :] * right_f[at, j]
            into[slot, i] = total.astype(BF16)
            return carry

        lax.fori_loop(0, block, one, 0)

    def gl_step(d):
        gl_block(d, gl_out, lax.rem(col + d, n))
        gl_copy(d).start()

    peers(gl_step)
    gl_block(0, gl_in, col)

    update = dot(mixed_b, out_w_ref[...])
    result_ref[...] = (switch_out * update).astype(BF16).reshape(block, block, width)
    grad_gate = (upstream * update * switch_out * (1.0 - switch_out)).astype(BF16)

    class Reduce:
        def __init__(self, src, into, mid, fin, sems):
            self.src, self.into, self.mid, self.fin = src, into, mid, fin
            self.s1, self.r1, self.s2, self.r2, self.s3, self.r3 = sems
            self.chunk = src.shape[1] - EXTRA

        def fill(self, parts, first, second):
            per = n // len(parts)
            for at, part in enumerate(parts):
                self.src[at * per : (at + 1) * per, : self.chunk] = part.astype(BF16).reshape(
                    per, self.chunk, part.shape[-1]
                )
            packed = pack_pair(first, second)
            for at in range(n):
                self.src[at, self.chunk :] = packed

        def copy_1(self, d):
            to_col = lax.rem(col + d, n)
            return remote(self.src.at[to_col], self.into.at[col], self.s1.at[d], self.r1.at[col], row, to_col)

        def copy_2(self, d):
            to_row = lax.rem(row + d, n)
            return remote(self.mid.at[row], self.mid.at[row], self.s2.at[d], self.r2.at[row], to_row, col)

        def copy_3(self, d):
            to_col = lax.rem(col + d, n)
            return remote(self.fin.at[col], self.fin.at[col], self.s3.at[d], self.r3.at[col], row, to_col)

        def start_1(self):
            peers(lambda d: self.copy_1(d).start())

        def total(self, buf):
            total = buf[0].astype(F32)
            for slot in range(1, n):
                total = total + buf[slot].astype(F32)
            return total[: self.chunk], unpack_pair(total[self.chunk :])

        def start_2(self):
            self.into[col] = self.src[col]
            peers(lambda d: arrived(self.into, self.r1, lax.rem(col + d, n)))
            body, (first, second) = self.total(self.into)
            self.mid[row, : self.chunk] = body.astype(BF16)
            self.mid[row, self.chunk :] = pack_pair(first, second)
            peers(lambda d: self.copy_2(d).start())

        def start_3(self):
            peers(lambda d: arrived(self.mid, self.r2, lax.rem(row + d, n)))
            body, norms = self.total(self.mid)
            self.fin[col] = body.astype(BF16)
            peers(lambda d: self.copy_3(d).start())
            return norms

        def finish(self, count):
            peers(lambda d: arrived(self.fin, self.r3, lax.rem(col + d, n)))
            per = n // count
            return [
                self.fin[at * per : (at + 1) * per].astype(F32).reshape(per * self.chunk, self.fin.shape[-1])
                for at in range(count)
            ]

        def drain(self):
            peers(lambda d: self.copy_1(d).wait_send())
            peers(lambda d: self.copy_2(d).wait_send())
            peers(lambda d: self.copy_3(d).wait_send())

    early = Reduce(a_src, a_in, a_mid, a_fin, (a1_send, a1_recv, a2_send, a2_recv, a3_send, a3_recv))
    late = Reduce(b_src, b_in, b_mid, b_fin, (b1_send, b1_recv, b2_send, b2_recv, b3_send, b3_recv))

    early.fill(
        [cell_sum(normed_b, grad_gate), cell_sum(mixed_b, grad_update)],
        jnp.sum(grad_mixed * scaled_mid, axis=0, keepdims=True),
        jnp.sum(grad_mixed, axis=0, keepdims=True),
    )
    early.start_1()
    grad_normed = dot_t(grad_gate, gate_w_ref[...])

    def gated_back(total, gate, values, switch):
        first = total * gate
        return first.astype(BF16), (first * values * (1.0 - switch)).astype(BF16)

    def slots(buf):
        total = buf[0].astype(F32)
        for slot in range(1, n):
            total = total + buf[slot].astype(F32)
        return total.reshape(cells, half)

    def gr_arrived(slot):
        @pl.when((row != col) | (slot != row))
        def _():
            arrived(gr_in, gr_recv, slot)

    peers(gr_arrived, 0)
    right_1, right_2 = gated_back(slots(gr_in), right_gate, right_values, right_switch)
    right_w = right_w_ref[...]
    grad_normed = grad_normed + dot_t(right_1, right_w[:, :half]) + dot_t(right_2, right_w[:, half:])

    peers(lambda d: arrived(gl_in, gl_recv, lax.rem(col + d, n)))
    left_1, left_2 = gated_back(slots(gl_in), left_gate, left_values, left_switch)
    left_w = left_w_ref[...]
    grad_normed = grad_normed + dot_t(left_1, left_w[:, :half]) + dot_t(left_2, left_w[:, half:])

    late.fill(
        [cell_sum(normed_b, left_1), cell_sum(normed_b, left_2), cell_sum(normed_b, right_1), cell_sum(normed_b, right_2)],
        jnp.sum(grad_normed * scaled_in, axis=0, keepdims=True),
        jnp.sum(grad_normed, axis=0, keepdims=True),
    )
    late.start_1()
    early.start_2()
    grad_pair_ref[...] = norm_back(grad_normed, in_gain, scaled_in, spread_in).reshape(block, block, width)
    late.start_2()
    norm_mid = early.start_3()
    norm_in = late.start_3()

    factor = 1.0 / (block * n)
    d_in_ref[0:1] = norm_in[0] * factor
    d_in_ref[1:2] = norm_in[1] * factor
    d_mid_ref[0:1] = norm_mid[0] * factor
    d_mid_ref[1:2] = norm_mid[1] * factor
    d_gate, d_out = early.finish(2)
    d_gate_ref[...] = d_gate * factor
    d_out_ref[...] = d_out * factor

    @pl.when(row != col)
    def _():
        right_copy(0).wait_send()
        gr_copy(0).wait_send()

    for copy in (right_copy, left_copy, gr_copy, gl_copy):
        peers(lambda d, copy=copy: copy(d).wait_send())
    parts = late.finish(4)
    d_left_ref[:, :half] = parts[0] * factor
    d_left_ref[:, half:] = parts[1] * factor
    d_right_ref[:, :half] = parts[2] * factor
    d_right_ref[:, half:] = parts[3] * factor
    early.drain()
    late.drain()


def solution(mesh):
    n = mesh.shape["row"]
    assert mesh.shape["col"] == n and n % 4 == 0

    def on_device(
        pair, cotangent, lengths, in_gain, in_bias, left_w, right_w, gate_w, mid_gain, mid_bias, out_w
    ):
        block, _, width = pair.shape
        half = left_w.shape[1] // 2
        vmem = pl.BlockSpec(memory_space=pltpu.VMEM)
        smem = pl.BlockSpec(memory_space=pltpu.SMEM)

        def blocks(dtype, *lead):
            return pltpu.VMEM(lead + (block, block, half), dtype)

        def reduce_bufs(rows):
            chunk = rows // n
            return [
                pltpu.VMEM((n, chunk + EXTRA, half), BF16),
                pltpu.VMEM((n, chunk + EXTRA, half), BF16),
                pltpu.VMEM((n, chunk + EXTRA, half), BF16),
                pltpu.VMEM((n, chunk, half), BF16),
            ]

        shape = jax.ShapeDtypeStruct
        return pl.pallas_call(
            functools.partial(kernel, n),
            out_shape=(
                shape(pair.shape, BF16),
                shape(pair.shape, F32),
                shape(left_w.shape, F32),
                shape(right_w.shape, F32),
                shape(gate_w.shape, F32),
                shape(out_w.shape, F32),
                shape((2, width), F32),
                shape((2, half), F32),
            ),
            in_specs=[smem] + [vmem] * 10,
            out_specs=[vmem] * 8,
            scratch_shapes=[
                blocks(BF16, n), blocks(BF16), blocks(BF16, n), blocks(F32, n), blocks(F32, n),
                blocks(F32), blocks(F32),
                blocks(BF16, n), blocks(BF16, n), blocks(BF16, n), blocks(BF16, n),
                *reduce_bufs(gate_w.shape[0] + out_w.shape[0]),
                *reduce_bufs(2 * (left_w.shape[0] + right_w.shape[0])),
            ]
            + [pltpu.SemaphoreType.DMA((n,))] * 20,
            compiler_params=pltpu.CompilerParams(
                collective_id=0, has_side_effects=True, vmem_limit_bytes=48 * 1024 * 1024
            ),
        )(
            lengths, pair, cotangent, in_gain.reshape(1, -1), in_bias.reshape(1, -1), left_w, right_w, gate_w,
            mid_gain.reshape(1, -1), mid_bias.reshape(1, -1), out_w,
        )

    cells = P(("grp", "row"), "col", None)
    return jax.shard_map(
        on_device,
        mesh=mesh,
        in_specs=(cells, cells, P("grp")) + (P(),) * 8,
        out_specs=(cells, cells) + (P("grp", None),) * 6,
        check_vma=False,
    )
```

```python
import functools

import jax
import jax.numpy as jnp
from jax import lax
from jax.experimental import pallas as pl
from jax.experimental.pallas import tpu as pltpu
from jax.sharding import PartitionSpec as P

EPS = 1e-05
MESH = pl.DeviceIdType.MESH
F32 = jnp.float32
BF16 = jnp.bfloat16
EXTRA = 16


def normalize(value, gain, bias):
    centre = value - jnp.mean(value, axis=-1, keepdims=True)
    spread = lax.rsqrt(jnp.mean(centre * centre, axis=-1, keepdims=True) + EPS)
    scaled = centre * spread
    return scaled * gain + bias, scaled, spread


def norm_back(upstream, gain, scaled, spread):
    inner = upstream * gain
    centred = inner - jnp.mean(inner, axis=-1, keepdims=True)
    return spread * (centred - scaled * jnp.mean(inner * scaled, axis=-1, keepdims=True))


def dot(a, b):
    return jnp.dot(a, b, preferred_element_type=F32)


def dot_t(a, b):
    return lax.dot_general(a, b, (((1,), (1,)), ((), ())), preferred_element_type=F32)


def cell_sum(a, b):
    return lax.dot_general(a, b, (((0,), (0,)), ((), ())), preferred_element_type=F32)


def pack_pair(first, second):
    place = lax.broadcasted_iota(jnp.int32, (EXTRA, first.shape[-1]), 0)
    lead_1, lead_2 = first.astype(BF16).astype(F32), second.astype(BF16).astype(F32)
    packed = jnp.where(place == 0, lead_1, 0.0)
    packed = jnp.where(place == 1, lead_2, packed)
    packed = jnp.where(place == 2, first - lead_1, packed)
    packed = jnp.where(place == 3, second - lead_2, packed)
    return packed.astype(BF16)


def unpack_pair(rows):
    return rows[0:1] + rows[2:3], rows[1:2] + rows[3:4]


def kernel(
    n,
    lengths_ref, pair_hbm, cot_hbm, in_gain_hbm, in_bias_hbm, left_w_hbm, right_w_hbm, gate_w_hbm,
    mid_gain_hbm, mid_bias_hbm, out_w_hbm,
    result_ref, grad_pair_ref, d_left_ref, d_right_ref, d_gate_ref, d_out_ref, d_in_ref, d_mid_ref,
    pair_ref, cot_ref, in_gain_ref, in_bias_ref, left_w_ref, right_w_ref, gate_w_ref,
    mid_gain_ref, mid_bias_ref, out_w_ref,
    left_f, right_buf, right_f, pp_out, pp_in, gp_buf, gp_f, gl_f, gr_out, gr_in,
    a_src, a_in, a_mid, a_fin, b_src, b_in, b_mid, b_fin,
    load_sem,
    r_send, r_recv, pp_send, pp_recv, gp_send, gp_recv, gr_send, gr_recv,
    a1_send, a1_recv, a2_send, a2_recv, a3_send, a3_recv,
    b1_send, b1_recv, b2_send, b2_recv, b3_send, b3_recv,
):
    block, _, width = pair_ref.shape
    half = out_w_ref.shape[0]
    cells = block * block
    row, col = lax.axis_index("row"), lax.axis_index("col")
    everyone = n * n

    def remote(src, dst, send, recv, to_row, to_col):
        return pltpu.make_async_remote_copy(
            src_ref=src, dst_ref=dst, send_sem=send, recv_sem=recv,
            device_id={"row": to_row, "col": to_col}, device_id_type=MESH,
        )

    def peers(body, first=1):
        def step(d, carry):
            body(d)
            return carry

        lax.fori_loop(first, n, step, 0)

    def arrived(buf, recv, slot):
        remote(buf.at[slot], buf.at[slot], recv.at[slot], recv.at[slot], row, col).wait_recv()

    loads = [
        pltpu.make_async_copy(src, dst, load_sem.at[at])
        for at, (src, dst) in enumerate(
            (
                (pair_hbm, pair_ref), (right_w_hbm, right_w_ref), (in_gain_hbm, in_gain_ref),
                (in_bias_hbm, in_bias_ref), (left_w_hbm, left_w_ref), (gate_w_hbm, gate_w_ref),
                (cot_hbm, cot_ref), (out_w_hbm, out_w_ref), (mid_gain_hbm, mid_gain_ref),
                (mid_bias_hbm, mid_bias_ref),
            )
        )
    ]
    for load in loads:
        load.start()
    barrier = pltpu.get_barrier_semaphore()

    def greet(d, carry):
        other = lax.rem(row * n + col + d, everyone)
        pl.semaphore_signal(
            barrier, inc=1, device_id={"row": other // n, "col": lax.rem(other, n)}, device_id_type=MESH
        )
        return carry

    lax.fori_loop(1, everyone, greet, 0)

    cell = lax.broadcasted_iota(jnp.int32, (cells, 1), 0)
    count = lengths_ref[0]
    mask = jnp.where(
        (row * block + cell // block < count) & (col * block + cell % block < count), 1.0, 0.0
    ).astype(F32)
    for load in loads[:4]:
        load.wait()
    in_gain, in_bias = in_gain_ref[...], in_bias_ref[...]
    normed, scaled_in, spread_in = normalize(
        pair_ref[...].reshape(cells, width).astype(F32), in_gain, in_bias
    )
    normed_b = normed.astype(BF16)

    right_all = dot(normed_b, right_w_ref[...])
    right_values, right_switch = right_all[:, :half], jax.nn.sigmoid(right_all[:, half:])
    right_gate = mask * right_switch
    right_buf[row] = (right_gate * right_values).astype(BF16).reshape(block, block, half)
    pl.semaphore_wait(barrier, everyone - 1)

    def right_copy(d):
        return remote(
            right_buf.at[row], right_buf.at[row], r_send.at[d], r_recv.at[row], lax.rem(row + d, n), col
        )

    peers(lambda d: right_copy(d).start())

    for load in loads[4:]:
        load.wait()
    left_all = dot(normed_b, left_w_ref[...])
    left_values, left_switch = left_all[:, :half], jax.nn.sigmoid(left_all[:, half:])
    left_gate = mask * left_switch
    left_f[...] = (left_gate * left_values).astype(BF16).astype(F32).reshape(block, block, half)

    switch_out = jax.nn.sigmoid(dot(normed_b, gate_w_ref[...]))
    upstream = cot_ref[...].reshape(cells, width).astype(F32)
    grad_update = (upstream * switch_out).astype(BF16)
    grad_mixed = dot_t(grad_update, out_w_ref[...])

    def pp_copy(to_col):
        return remote(pp_out.at[to_col], pp_in.at[col], pp_send.at[to_col], pp_recv.at[col], row, to_col)

    def product_block(d, wait):
        at = lax.rem(row + d, n)
        if wait:
            arrived(right_buf, r_recv, at)
        right_f[at] = right_buf[at].astype(F32)

        def one(i, carry):
            near = left_f[i]
            rows = [jnp.sum(near * right_f[at, j], axis=0, keepdims=True) for j in range(block)]
            pp_out[at, i] = jnp.concatenate(rows, axis=0).astype(BF16)
            return carry

        lax.fori_loop(0, block, one, 0)

        @pl.when(at != col)
        def _():
            pp_copy(at).start()

    product_block(0, False)
    peers(lambda d: product_block(d, True))

    def summed(own, buf, first):
        def step(d, total):
            slot = lax.rem(first + d, n)
            return total + buf[slot].astype(F32)

        return lax.fori_loop(1, n, step, own.astype(F32)).reshape(cells, half)

    peers(lambda d: arrived(pp_in, pp_recv, lax.rem(col + d, n)))
    product = summed(pp_out[col], pp_in, col)
    mid_gain = mid_gain_ref[...]
    mixed, scaled_mid, spread_mid = normalize(product, mid_gain, mid_bias_ref[...])
    grad_prod = norm_back(grad_mixed, mid_gain, scaled_mid, spread_mid)
    gp_buf[col] = grad_prod.astype(BF16).reshape(block, block, half)

    def gp_copy(d):
        return remote(
            gp_buf.at[col], gp_buf.at[col], gp_send.at[d], gp_recv.at[col], row, lax.rem(col + d, n)
        )

    peers(lambda d: gp_copy(d).start())

    def gr_copy(to_row):
        return remote(gr_out.at[to_row], gr_in.at[row], gr_send.at[to_row], gr_recv.at[row], to_row, col)

    def gr_block(d, wait):
        at = lax.rem(col + d, n)
        if wait:
            arrived(gp_buf, gp_recv, at)
        gp_f[at] = gp_buf[at].astype(F32)

        def one(j, carry):
            total = gp_f[at, 0, pl.ds(j, 1), :] * left_f[0]
            for i in range(1, block):
                total = total + gp_f[at, i, pl.ds(j, 1), :] * left_f[i]
            gr_out[at, j] = total.astype(BF16)
            return carry

        lax.fori_loop(0, block, one, 0)

        @pl.when(at != row)
        def _():
            gr_copy(at).start()

    gr_block(0, False)

    mixed_b = mixed.astype(BF16)
    update = dot(mixed_b, out_w_ref[...])
    result_ref[...] = (switch_out * update).astype(BF16).reshape(block, block, width)
    grad_gate = (upstream * update * switch_out * (1.0 - switch_out)).astype(BF16)

    peers(lambda d: gr_block(d, True))

    def gl_row(i, carry):
        def step(at, total):
            for j in range(block):
                total = total + gp_f[at, i, j : j + 1, :] * right_f[at, j]
            return total

        gl_f[i] = lax.fori_loop(0, n, step, jnp.zeros((block, half), F32))
        return carry

    lax.fori_loop(0, block, gl_row, 0)

    def gated_back(total, gate, values, switch):
        first = total * gate
        return first.astype(BF16), (first * values * (1.0 - switch)).astype(BF16)

    left_1, left_2 = gated_back(gl_f[...].reshape(cells, half), left_gate, left_values, left_switch)

    class Reduce:
        def __init__(self, src, into, mid, fin, sems):
            self.src, self.into, self.mid, self.fin = src, into, mid, fin
            self.s1, self.r1, self.s2, self.r2, self.s3, self.r3 = sems
            self.chunk = src.shape[1] - EXTRA

        def fill(self, parts, first, second):
            per = n // len(parts)
            for at, part in enumerate(parts):
                self.src[at * per : (at + 1) * per, : self.chunk] = part.astype(BF16).reshape(
                    per, self.chunk, part.shape[-1]
                )
            packed = pack_pair(first, second)
            for at in range(n):
                self.src[at, self.chunk :] = packed

        def copy_1(self, d):
            to_col = lax.rem(col + d, n)
            return remote(self.src.at[to_col], self.into.at[col], self.s1.at[d], self.r1.at[col], row, to_col)

        def copy_2(self, d):
            to_row = lax.rem(row + d, n)
            return remote(self.mid.at[row], self.mid.at[row], self.s2.at[d], self.r2.at[row], to_row, col)

        def copy_3(self, d):
            to_col = lax.rem(col + d, n)
            return remote(self.fin.at[col], self.fin.at[col], self.s3.at[d], self.r3.at[col], row, to_col)

        def start_1(self):
            peers(lambda d: self.copy_1(d).start())

        def total(self, buf):
            total = buf[0].astype(F32)
            for slot in range(1, n):
                total = total + buf[slot].astype(F32)
            return total[: self.chunk], unpack_pair(total[self.chunk :])

        def start_2(self):
            self.into[col] = self.src[col]
            peers(lambda d: arrived(self.into, self.r1, lax.rem(col + d, n)))
            body, (first, second) = self.total(self.into)
            self.mid[row, : self.chunk] = body.astype(BF16)
            self.mid[row, self.chunk :] = pack_pair(first, second)
            peers(lambda d: self.copy_2(d).start())

        def start_3(self):
            peers(lambda d: arrived(self.mid, self.r2, lax.rem(row + d, n)))
            body, norms = self.total(self.mid)
            self.fin[col] = body.astype(BF16)
            peers(lambda d: self.copy_3(d).start())
            return norms

        def finish(self, count):
            peers(lambda d: arrived(self.fin, self.r3, lax.rem(col + d, n)))
            per = n // count
            return [
                self.fin[at * per : (at + 1) * per].astype(F32).reshape(per * self.chunk, self.fin.shape[-1])
                for at in range(count)
            ]

        def drain(self):
            peers(lambda d: self.copy_1(d).wait_send())
            peers(lambda d: self.copy_2(d).wait_send())
            peers(lambda d: self.copy_3(d).wait_send())

    early = Reduce(a_src, a_in, a_mid, a_fin, (a1_send, a1_recv, a2_send, a2_recv, a3_send, a3_recv))
    late = Reduce(b_src, b_in, b_mid, b_fin, (b1_send, b1_recv, b2_send, b2_recv, b3_send, b3_recv))

    early.fill(
        [
            cell_sum(normed_b, grad_gate), cell_sum(mixed_b, grad_update),
            cell_sum(normed_b, left_1), cell_sum(normed_b, left_2),
        ],
        jnp.sum(grad_mixed * scaled_mid, axis=0, keepdims=True),
        jnp.sum(grad_mixed, axis=0, keepdims=True),
    )
    early.start_1()
    left_w, right_w = left_w_ref[...], right_w_ref[...]
    grad_normed = dot_t(grad_gate, gate_w_ref[...])
    grad_normed = grad_normed + dot_t(left_1, left_w[:, :half]) + dot_t(left_2, left_w[:, half:])

    peers(lambda d: arrived(gr_in, gr_recv, lax.rem(row + d, n)))
    grad_right = summed(gr_out[row], gr_in, row)
    right_1, right_2 = gated_back(grad_right, right_gate, right_values, right_switch)
    grad_normed = grad_normed + dot_t(right_1, right_w[:, :half]) + dot_t(right_2, right_w[:, half:])

    late.fill(
        [cell_sum(normed_b, right_1), cell_sum(normed_b, right_2)],
        jnp.sum(grad_normed * scaled_in, axis=0, keepdims=True),
        jnp.sum(grad_normed, axis=0, keepdims=True),
    )
    late.start_1()
    early.start_2()
    grad_pair_ref[...] = norm_back(grad_normed, in_gain, scaled_in, spread_in).reshape(block, block, width)
    late.start_2()
    norm_mid = early.start_3()
    norm_in = late.start_3()

    factor = 1.0 / (block * n)
    d_in_ref[0:1] = norm_in[0] * factor
    d_in_ref[1:2] = norm_in[1] * factor
    d_mid_ref[0:1] = norm_mid[0] * factor
    d_mid_ref[1:2] = norm_mid[1] * factor
    parts = early.finish(4)
    d_gate_ref[...] = parts[0] * factor
    d_out_ref[...] = parts[1] * factor
    d_left_ref[:, :half] = parts[2] * factor
    d_left_ref[:, half:] = parts[3] * factor

    for copy in (right_copy, gp_copy):
        peers(lambda d, copy=copy: copy(d).wait_send())
    peers(lambda d: pp_copy(lax.rem(col + d, n)).wait_send())
    peers(lambda d: gr_copy(lax.rem(row + d, n)).wait_send())
    parts = late.finish(2)
    d_right_ref[:, :half] = parts[0] * factor
    d_right_ref[:, half:] = parts[1] * factor
    early.drain()
    late.drain()


def write_out(*refs):
    sem = refs[-1]
    count = len(refs) // 2
    copies = [
        pltpu.make_async_copy(src, dst, sem.at[at])
        for at, (src, dst) in enumerate(zip(refs[:count], refs[count : 2 * count]))
    ]
    for copy in copies:
        copy.start()
    for copy in copies:
        copy.wait()


def solution(mesh):
    n = mesh.shape["row"]
    assert mesh.shape["col"] == n and n % 4 == 0

    def on_device(
        pair, cotangent, lengths, in_gain, in_bias, left_w, right_w, gate_w, mid_gain, mid_bias, out_w
    ):
        block, _, width = pair.shape
        half = left_w.shape[1] // 2
        vmem = pl.BlockSpec(memory_space=pltpu.VMEM)
        smem = pl.BlockSpec(memory_space=pltpu.SMEM)
        hbm = pl.BlockSpec(memory_space=pltpu.HBM)
        operands = [
            pair, cotangent, in_gain.reshape(1, -1), in_bias.reshape(1, -1), left_w, right_w, gate_w,
            mid_gain.reshape(1, -1), mid_bias.reshape(1, -1), out_w,
        ]

        def blocks(dtype, *lead):
            return pltpu.VMEM(lead + (block, block, half), dtype)

        def reduce_bufs(rows):
            chunk = rows // n
            return [
                pltpu.VMEM((n, chunk + EXTRA, half), BF16),
                pltpu.VMEM((n, chunk + EXTRA, half), BF16),
                pltpu.VMEM((n, chunk + EXTRA, half), BF16),
                pltpu.VMEM((n, chunk, half), BF16),
            ]

        shape = jax.ShapeDtypeStruct
        out_shape = (
            shape(pair.shape, BF16),
            shape(pair.shape, F32),
            shape(left_w.shape, F32),
            shape(right_w.shape, F32),
            shape(gate_w.shape, F32),
            shape(out_w.shape, F32),
            shape((2, width), F32),
            shape((2, half), F32),
        )
        outs = pl.pallas_call(
            functools.partial(kernel, n),
            out_shape=out_shape,
            in_specs=[smem] + [hbm] * 10,
            out_specs=[vmem] * 8,
            scratch_shapes=[
                *[pltpu.VMEM(x.shape, x.dtype) for x in operands],
                blocks(F32), blocks(BF16, n), blocks(F32, n), blocks(BF16, n), blocks(BF16, n),
                blocks(BF16, n), blocks(F32, n), blocks(F32), blocks(BF16, n), blocks(BF16, n),
                *reduce_bufs(gate_w.shape[0] + out_w.shape[0] + 2 * left_w.shape[0]),
                *reduce_bufs(2 * right_w.shape[0]),
                pltpu.SemaphoreType.DMA((10,)),
            ]
            + [pltpu.SemaphoreType.DMA((n,))] * 20,
            compiler_params=pltpu.CompilerParams(
                collective_id=0, has_side_effects=True, vmem_limit_bytes=63 * 1024 * 1024
            ),
        )(lengths, *operands)
        return pl.pallas_call(
            write_out,
            out_shape=out_shape,
            in_specs=[vmem] * 8,
            out_specs=[hbm] * 8,
            scratch_shapes=[pltpu.SemaphoreType.DMA((8,))],
        )(*outs)

    cells = P(("grp", "row"), "col", None)
    return jax.shard_map(
        on_device,
        mesh=mesh,
        in_specs=(cells, cells, P("grp")) + (P(),) * 8,
        out_specs=(cells, cells) + (P("grp", None),) * 6,
        check_vma=False,
    )
```

```python
import functools

import jax
import jax.numpy as jnp
from jax import lax
from jax.experimental import pallas as pl
from jax.experimental.pallas import tpu as pltpu
from jax.sharding import PartitionSpec as P

EPS = 1e-05
MESH = pl.DeviceIdType.MESH
F32 = jnp.float32
BF16 = jnp.bfloat16
ROWS = 16


def normalize(value, gain, bias):
    centre = value - jnp.mean(value, axis=-1, keepdims=True)
    spread = lax.rsqrt(jnp.mean(centre * centre, axis=-1, keepdims=True) + EPS)
    scaled = centre * spread
    return scaled * gain + bias, scaled, spread


def norm_back(upstream, gain, scaled, spread):
    inner = upstream * gain
    centred = inner - jnp.mean(inner, axis=-1, keepdims=True)
    return spread * (centred - scaled * jnp.mean(inner * scaled, axis=-1, keepdims=True))


def dot(a, b):
    return jnp.dot(a, b, preferred_element_type=F32)


def dot_t(a, b):
    return lax.dot_general(a, b, (((1,), (1,)), ((), ())), preferred_element_type=F32)


def cell_sum(a, b):
    return lax.dot_general(a, b, (((0,), (0,)), ((), ())), preferred_element_type=F32)


def kernel(
    n,
    lengths_ref, pair_hbm, cot_hbm, in_gain_hbm, in_bias_hbm, left_w_hbm, right_w_hbm, gate_w_hbm,
    mid_gain_hbm, mid_bias_hbm, out_w_hbm,
    result_ref, grad_pair_ref, d_left_ref, d_right_ref, d_gate_ref, d_out_ref, d_in_ref, d_mid_ref,
    pair_ref, cot_ref, in_gain_ref, in_bias_ref, left_w_ref, right_w_ref, gate_w_ref,
    mid_gain_ref, mid_bias_ref, out_w_ref,
    left_f, right_buf, right_f, pp_out, pp_in, gp_buf, gp_f, gl_f, gr_out, gr_in,
    load_sem,
    r_send, r_recv, pp_send, pp_recv, gp_send, gp_recv, gr_send, gr_recv,
    norm_buf, norm_sems,
    *sums_refs,
):
    block, _, width = pair_ref.shape
    half = out_w_ref.shape[0]
    cells = block * block
    row, col = lax.axis_index("row"), lax.axis_index("col")

    def remote(src, dst, send, recv, to_row, to_col):
        return pltpu.make_async_remote_copy(
            src_ref=src, dst_ref=dst, send_sem=send, recv_sem=recv,
            device_id={"row": to_row, "col": to_col}, device_id_type=MESH,
        )

    def wrap(place):
        return jnp.where(place >= n, place - n, place)

    def peers(body, first=1):
        def step(d, carry):
            body(d)
            return carry

        lax.fori_loop(first, n, step, 0, unroll=n <= 4)

    chip = col // 2
    core = col - 2 * chip

    def near_row(d):
        both = jnp.minimum(row, n - 1 - row)
        paired = row + (2 * (d % 2) - 1) * ((d + 1) // 2)
        alone = jnp.where(row < n - 1 - row, row + d - both, row - d + both)
        return jnp.where(d <= 2 * both, paired, alone)

    def near_col(d):
        along = chip + d // 2
        along = jnp.where(along >= n // 2, along - n // 2, along)
        swap = d % 2
        return along * 2 + core + swap - 2 * core * swap

    def arrived(buf, recv, slot):
        remote(buf.at[slot], buf.at[slot], recv.at[slot], recv.at[slot], row, col).wait_recv()

    loads = [
        pltpu.make_async_copy(src, dst, load_sem.at[at])
        for at, (src, dst) in enumerate(
            (
                (pair_hbm, pair_ref), (right_w_hbm, right_w_ref), (in_gain_hbm, in_gain_ref),
                (in_bias_hbm, in_bias_ref), (left_w_hbm, left_w_ref), (gate_w_hbm, gate_w_ref),
                (cot_hbm, cot_ref), (out_w_hbm, out_w_ref), (mid_gain_hbm, mid_gain_ref),
                (mid_bias_hbm, mid_bias_ref),
            )
        )
    ]
    for load in loads:
        load.start()
    barrier = pltpu.get_barrier_semaphore()

    everyone = n * n
    me = row * n + col

    def others(body):
        def one_row(d_row, first):
            to_row = wrap(row + d_row)

            def step(d_col, carry):
                to_col = wrap(col + d_col)
                body(to_row * n + to_col, to_row, to_col)
                return carry

            lax.fori_loop(first, n, step, 0, unroll=n <= 4)

        def step_row(d_row, carry):
            one_row(d_row, 0)
            return carry

        lax.fori_loop(1, n, step_row, 0, unroll=n <= 4)
        one_row(0, 1)

    def greet(other, to_row, to_col):
        pl.semaphore_signal(
            barrier, inc=1, device_id={"row": to_row, "col": to_col}, device_id_type=MESH
        )

    others(greet)

    cell = lax.broadcasted_iota(jnp.int32, (cells, 1), 0)
    count = lengths_ref[0]
    mask = jnp.where(
        (row * block + cell // block < count) & (col * block + cell % block < count), 1.0, 0.0
    ).astype(F32)
    for load in loads[:4]:
        load.wait()
    in_gain, in_bias = in_gain_ref[...], in_bias_ref[...]
    normed, scaled_in, spread_in = normalize(
        pair_ref[...].reshape(cells, width).astype(F32), in_gain, in_bias
    )
    normed_b = normed.astype(BF16)

    right_all = dot(normed_b, right_w_ref[...])
    right_values, right_switch = right_all[:, :half], jax.nn.sigmoid(right_all[:, half:])
    right_gate = mask * right_switch
    right_buf[row] = (right_gate * right_values).astype(BF16).reshape(block, block, half)
    pl.semaphore_wait(barrier, everyone - 1)

    def right_copy(d):
        return remote(
            right_buf.at[row], right_buf.at[row], r_send.at[d], r_recv.at[row], wrap(row + d), col
        )

    peers(lambda d: right_copy(d).start())

    for load in loads[4:]:
        load.wait()
    left_all = dot(normed_b, left_w_ref[...])
    left_values, left_switch = left_all[:, :half], jax.nn.sigmoid(left_all[:, half:])
    left_gate = mask * left_switch
    left_f[...] = (left_gate * left_values).astype(BF16).astype(F32).reshape(block, block, half)

    switch_out = jax.nn.sigmoid(dot(normed_b, gate_w_ref[...]))
    upstream = cot_ref[...].reshape(cells, width).astype(F32)
    grad_update = (upstream * switch_out).astype(BF16)
    grad_mixed = dot_t(grad_update, out_w_ref[...])

    def pp_copy(to_col):
        return remote(pp_out.at[to_col], pp_in.at[col], pp_send.at[to_col], pp_recv.at[col], row, to_col)

    def product_block(d, wait):
        at = near_row(d) if wait else row
        if wait:
            arrived(right_buf, r_recv, at)
        right_f[at] = right_buf[at].astype(F32)

        def one(i, carry):
            near = left_f[i]
            rows = [jnp.sum(near * right_f[at, j], axis=0, keepdims=True) for j in range(block)]
            pp_out[at, i] = jnp.concatenate(rows, axis=0).astype(BF16)
            return carry

        lax.fori_loop(0, block, one, 0)

        @pl.when(at != col)
        def _():
            pp_copy(at).start()

    product_block(0, False)
    peers(lambda d: product_block(d, True))

    def summed(own, buf, first):
        def step(d, total):
            slot = wrap(first + d)
            return total + buf[slot].astype(F32)

        return lax.fori_loop(1, n, step, own.astype(F32)).reshape(cells, half)

    peers(lambda d: arrived(pp_in, pp_recv, wrap(col + d)))
    product = summed(pp_out[col], pp_in, col)
    mid_gain = mid_gain_ref[...]
    mixed, scaled_mid, spread_mid = normalize(product, mid_gain, mid_bias_ref[...])
    grad_prod = norm_back(grad_mixed, mid_gain, scaled_mid, spread_mid)
    gp_buf[col] = grad_prod.astype(BF16).reshape(block, block, half)

    def gp_copy(d):
        return remote(
            gp_buf.at[col], gp_buf.at[col], gp_send.at[d], gp_recv.at[col], row, wrap(col + d)
        )

    peers(lambda d: gp_copy(d).start())

    def gr_copy(to_row):
        return remote(gr_out.at[to_row], gr_in.at[row], gr_send.at[to_row], gr_recv.at[row], to_row, col)

    def gr_block(d, wait):
        at = near_col(d) if wait else col
        if wait:
            arrived(gp_buf, gp_recv, at)
        gp_f[at] = gp_buf[at].astype(F32)

        def one(j, carry):
            total = gp_f[at, 0, pl.ds(j, 1), :] * left_f[0]
            for i in range(1, block):
                total = total + gp_f[at, i, pl.ds(j, 1), :] * left_f[i]
            gr_out[at, j] = total.astype(BF16)
            return carry

        lax.fori_loop(0, block, one, 0)

        @pl.when(at != row)
        def _():
            gr_copy(at).start()

    class Direct:
        def __init__(self, src, into, fin, sems):
            self.src, self.into, self.fin, self.sems = src, into, fin, sems

        def fill(self, parts):
            per = everyone // len(parts)
            for at, part in enumerate(parts):
                self.src[at * per : (at + 1) * per] = part.astype(BF16).reshape(
                    per, self.src.shape[1], part.shape[-1]
                )

        def start_1(self):
            others(
                lambda other, *to: remote(
                    self.src.at[other], self.into.at[me], self.sems.at[0], self.sems.at[1], *to
                ).start()
            )

        def all_but_one(self, send, recv):
            rest = self.into.at[0 : everyone - 1]
            return remote(rest, rest, self.sems.at[send], self.sems.at[recv], row, col)

        def start_2(self):
            self.into[me] = self.src[me]
            self.all_but_one(0, 1).wait_recv()
            self.fin[me] = jnp.sum(self.into[...].astype(F32), axis=0).astype(BF16)
            others(
                lambda other, *to: remote(
                    self.fin.at[me], self.fin.at[me], self.sems.at[2], self.sems.at[3], *to
                ).start()
            )

        def start_3(self):
            pass

        def finish(self, count):
            self.all_but_one(2, 3).wait_recv()
            per = everyone // count
            chunk, lanes = self.fin.shape[1:]
            return [
                self.fin[at * per : (at + 1) * per].astype(F32).reshape(per * chunk, lanes)
                for at in range(count)
            ]

        def drain(self):
            self.all_but_one(0, 1).wait_send()
            self.all_but_one(2, 3).wait_send()

    class Staged:
        def __init__(self, src, into, mid, fin, sems):
            self.src, self.into, self.mid, self.fin, self.sems = src, into, mid, fin, sems
            self.chunk = fin.shape[1]

        def fill(self, parts):
            per = n // len(parts)
            for at, part in enumerate(parts):
                self.src[at * per : (at + 1) * per] = part.astype(BF16).reshape(
                    per, self.chunk, part.shape[-1]
                )

        def copy_1(self, d):
            to_col = wrap(col + d)
            return remote(
                self.src.at[to_col], self.into.at[col], self.sems.at[0], self.sems.at[1], row, to_col
            )

        def copy_2(self, d):
            to_row = wrap(row + d)
            return remote(
                self.mid.at[row], self.mid.at[row], self.sems.at[2], self.sems.at[3], to_row, col
            )

        def copy_3(self, d):
            to_col = wrap(col + d)
            return remote(
                self.fin.at[col], self.fin.at[col], self.sems.at[4], self.sems.at[5], row, to_col
            )

        def all_but_one(self, send, recv):
            rest = self.fin.at[0 : n - 1]
            return remote(rest, rest, self.sems.at[send], self.sems.at[recv], row, col)

        def start_1(self):
            peers(lambda d: self.copy_1(d).start())

        def start_2(self):
            self.into[col] = self.src[col]
            self.all_but_one(0, 1).wait_recv()
            self.mid[row] = jnp.sum(self.into[...].astype(F32), axis=0).astype(BF16)
            peers(lambda d: self.copy_2(d).start())

        def start_3(self):
            self.all_but_one(2, 3).wait_recv()
            self.fin[col] = jnp.sum(self.mid[...].astype(F32), axis=0).astype(BF16)
            peers(lambda d: self.copy_3(d).start())

        def finish(self, count):
            self.all_but_one(4, 5).wait_recv()
            per = n // count
            return [
                self.fin[at * per : (at + 1) * per].astype(F32).reshape(per * self.chunk, self.fin.shape[-1])
                for at in range(count)
            ]

        def drain(self):
            for at in (0, 2, 4):
                self.all_but_one(at, at + 1).wait_send()

    sums_a, sums_b = Staged(*sums_refs[0:5]), Staged(*sums_refs[5:10])
    sums_c = (Direct if len(sums_refs) == 14 else Staged)(*sums_refs[10:])

    gr_block(0, False)

    mixed_b = mixed.astype(BF16)
    update = dot(mixed_b, out_w_ref[...])
    result_ref[...] = (switch_out * update).astype(BF16).reshape(block, block, width)
    grad_gate = (upstream * update * switch_out * (1.0 - switch_out)).astype(BF16)

    peers(lambda d: gr_block(d, True))
    sums_a.fill([cell_sum(normed_b, grad_gate), cell_sum(mixed_b, grad_update)])
    sums_a.start_1()

    def gl_row(i, carry):
        def step(at, total):
            for j in range(block):
                total = total + gp_f[at, i, j : j + 1, :] * right_f[at, j]
            return total

        gl_f[i] = lax.fori_loop(0, n, step, jnp.zeros((block, half), F32))
        return carry

    lax.fori_loop(0, block, gl_row, 0)

    def gated_back(total, gate, values, switch):
        first = total * gate
        return first.astype(BF16), (first * values * (1.0 - switch)).astype(BF16)

    left_1, left_2 = gated_back(gl_f[...].reshape(cells, half), left_gate, left_values, left_switch)

    sums_b.fill([cell_sum(normed_b, left_1), cell_sum(normed_b, left_2)])
    sums_b.start_1()
    left_w, right_w = left_w_ref[...], right_w_ref[...]
    grad_normed = dot_t(grad_gate, gate_w_ref[...])
    grad_normed = grad_normed + dot_t(left_1, left_w[:, :half]) + dot_t(left_2, left_w[:, half:])
    sums_a.start_2()

    peers(lambda d: arrived(gr_in, gr_recv, wrap(row + d)))
    grad_right = summed(gr_out[row], gr_in, row)
    right_1, right_2 = gated_back(grad_right, right_gate, right_values, right_switch)
    sums_c.fill([cell_sum(normed_b, right_1), cell_sum(normed_b, right_2)])
    sums_c.start_1()

    grad_normed = grad_normed + dot_t(right_1, right_w[:, :half]) + dot_t(right_2, right_w[:, half:])

    place = lax.broadcasted_iota(jnp.int32, (8, width), 0)
    own = jnp.zeros((8, width), F32)
    for at, term in enumerate((grad_normed * scaled_in, grad_normed, grad_mixed * scaled_mid, grad_mixed)):
        own = jnp.where(place == at, jnp.sum(term, axis=0, keepdims=True), own)
    norm_buf[me] = own
    others(
        lambda other, *to: remote(
            norm_buf.at[me], norm_buf.at[me], norm_sems.at[0], norm_sems.at[1], *to
        ).start()
    )
    sums_b.start_2()
    sums_a.start_3()
    sums_c.start_2()
    grad_pair_ref[...] = norm_back(grad_normed, in_gain, scaled_in, spread_in).reshape(block, block, width)
    sums_b.start_3()
    sums_c.start_3()

    factor = 1.0 / (block * n)
    parts = sums_a.finish(2)
    d_gate_ref[...] = parts[0] * factor
    d_out_ref[...] = parts[1] * factor
    parts = sums_b.finish(2)
    d_left_ref[:, :half] = parts[0] * factor
    d_left_ref[:, half:] = parts[1] * factor
    rest = norm_buf.at[0 : everyone - 1]
    rest_copy = remote(rest, rest, norm_sems.at[0], norm_sems.at[1], row, col)
    rest_copy.wait_recv()
    norms = jnp.sum(norm_buf[...], axis=0) * factor
    d_in_ref[...] = norms[0:2]
    d_mid_ref[...] = norms[2:4]
    rest_copy.wait_send()

    for copy in (right_copy, gp_copy):
        peers(lambda d, copy=copy: copy(d).wait_send())
    peers(lambda d: pp_copy(wrap(col + d)).wait_send())
    peers(lambda d: gr_copy(wrap(row + d)).wait_send())
    sums_a.drain()
    sums_b.drain()
    parts = sums_c.finish(2)
    d_right_ref[:, :half] = parts[0] * factor
    d_right_ref[:, half:] = parts[1] * factor
    sums_c.drain()


def write_out(*refs):
    sem = refs[-1]
    count = len(refs) // 2
    copies = [
        pltpu.make_async_copy(src, dst, sem.at[at])
        for at, (src, dst) in enumerate(zip(refs[:count], refs[count : 2 * count]))
    ]
    for copy in copies:
        copy.start()
    for copy in copies:
        copy.wait()


def solution(mesh):
    n = mesh.shape["row"]
    assert mesh.shape["col"] == n and n % 4 == 0

    def on_device(
        pair, cotangent, lengths, in_gain, in_bias, left_w, right_w, gate_w, mid_gain, mid_bias, out_w
    ):
        block, _, width = pair.shape
        half = left_w.shape[1] // 2
        vmem = pl.BlockSpec(memory_space=pltpu.VMEM)
        smem = pl.BlockSpec(memory_space=pltpu.SMEM)
        hbm = pl.BlockSpec(memory_space=pltpu.HBM)
        operands = [
            pair, cotangent, in_gain.reshape(1, -1), in_bias.reshape(1, -1), left_w, right_w, gate_w,
            mid_gain.reshape(1, -1), mid_bias.reshape(1, -1), out_w,
        ]

        def blocks(dtype, *lead):
            return pltpu.VMEM(lead + (block, block, half), dtype)

        def reduce_bufs(rows, direct=False):
            sems = pltpu.SemaphoreType.DMA((6,))
            share = rows // (n * n)
            if direct and share % ROWS == 0:
                return [pltpu.VMEM((n * n, share, half), BF16)] * 3 + [sems]
            return [pltpu.VMEM((n, rows // n, half), BF16)] * 4 + [sems]

        shape = jax.ShapeDtypeStruct
        out_shape = (
            shape(pair.shape, BF16),
            shape(pair.shape, F32),
            shape(left_w.shape, F32),
            shape(right_w.shape, F32),
            shape(gate_w.shape, F32),
            shape(out_w.shape, F32),
            shape((2, width), F32),
            shape((2, half), F32),
        )
        outs = pl.pallas_call(
            functools.partial(kernel, n),
            out_shape=out_shape,
            in_specs=[smem] + [hbm] * 10,
            out_specs=[vmem] * 8,
            scratch_shapes=[
                *[pltpu.VMEM(x.shape, x.dtype) for x in operands],
                blocks(F32), blocks(BF16, n), blocks(F32, n), blocks(BF16, n), blocks(BF16, n),
                blocks(BF16, n), blocks(F32, n), blocks(F32), blocks(BF16, n), blocks(BF16, n),
                pltpu.SemaphoreType.DMA((10,)),
                *[pltpu.SemaphoreType.DMA((n,))] * 8,
                pltpu.VMEM((n * n, 8, width), F32),
                pltpu.SemaphoreType.DMA((2,)),
                *reduce_bufs(gate_w.shape[0] + out_w.shape[0]),
                *reduce_bufs(2 * left_w.shape[0]),
                *reduce_bufs(2 * right_w.shape[0], direct=True),
            ],
            compiler_params=pltpu.CompilerParams(
                collective_id=0, has_side_effects=True, vmem_limit_bytes=63 * 1024 * 1024
            ),
        )(lengths, *operands)
        return pl.pallas_call(
            write_out,
            out_shape=out_shape,
            in_specs=[vmem] * 8,
            out_specs=[hbm] * 8,
            scratch_shapes=[pltpu.SemaphoreType.DMA((8,))],
        )(*outs)

    cells = P(("grp", "row"), "col", None)
    return jax.shard_map(
        on_device,
        mesh=mesh,
        in_specs=(cells, cells, P("grp")) + (P(),) * 8,
        out_specs=(cells, cells) + (P("grp", None),) * 6,
        check_vma=False,
    )
```
